256 devices in a mesh: lag: 8 (over x, z_hi), space: 32 (over z_lo, y, core).
Axes of the slice: x: 4, y: 4, z: 8 (z_hi: 2, z_lo: 4; z = z_hi * 4 + z_lo), core: 2. Of those that a mesh axis runs over, the one named last changes fastest.
Arguments:
- lagged: bfloat16 [8, 5120, 136, 128], P('lag', 'space')
- weights: float32 [2048, 128, 128], P(('space', 'lag'))
- cell_index: int32 [5120], P('space'), may hold values from 0 to 64, as said below
- fraction: float32 [5120], P('space'), may hold values from 0.05 to 0.95
Outputs:
- smoothed: bfloat16 [8, 5120, 136, 128], P('lag', 'space')
The draws below stay inside these ranges and needn't reach their ends.
Inputs may be any that keep to these rules, and one draw needn't show every extreme that they name: `cell_index`: within each block of 160 columns of one index of space, the first column has cell 0 and the second cell 64.
All inputs are finite; a program needn't handle non-finite values.
Results may differ from the reference program's by a relative error of at most 0.0057.
Values may be sent and summed in bfloat16 or wider, within the bound.
No kernel may reach another device: no remote copies, remote signals or barrier semaphores. Data moves between devices by JAX's collectives and lax.ppermute only.
A program may use at most 128 MiB of HBM per device.

```python
import jax
import jax.numpy as jnp
from jax import lax

K = 128
LEV = 136
COLS = 160
LAGS = 8
GS = 64
GC = 2048
NCOL = 5120


def draw_lagged(key, part):
    key = jax.random.fold_in(key, 23)
    key_mean, key_member = jax.random.split(key, 2)
    center = jax.random.normal(key_mean, (LAGS, NCOL, LEV, 1), jnp.float32)
    members = jax.random.normal(key_member, (LAGS, NCOL, LEV, K), jnp.float32)
    return (center + members).astype(jnp.bfloat16)


def draw_weights(key, part):
    key = jax.random.fold_in(key, 11)
    key_diag, key_rough = jax.random.split(key, 2)
    identity = jnp.eye(K, dtype=jnp.float32)
    diagonal = jax.random.uniform(key_diag, (GC, K, 1), jnp.float32, 0.5, 1.5)
    rough = 0.1 * jax.random.normal(key_rough, (GC, K, K), jnp.float32)
    return (diagonal * identity + rough).astype(jnp.float32)


def draw_cell_index(key, part):
    key = jax.random.fold_in(key, 37)
    blocks = NCOL // COLS
    member_values = jax.random.randint(key, (blocks, COLS), 0, GS + 1, dtype=jnp.int32)
    member_values = member_values.at[:, 0].set(0)
    member_values = member_values.at[:, 1].set(GS)
    return member_values.reshape(NCOL)


def block_scale(key, extent, cuts, smallest, top_value):
    def one(dim, blocks):
        draws = jax.random.uniform(jax.random.fold_in(jax.random.fold_in(key, 6), dim), (blocks,), jnp.float32, smallest / len(cuts), top_value / len(cuts))
        return jnp.repeat(jnp.exp(draws), extent[dim] // blocks).reshape((-1,) + (1,) * (len(extent) - dim - 1))

    loudness = one(*cuts[0])
    for cut in cuts[1:]:
        loudness = loudness * one(*cut)
    return loudness


def setup_inputs(seed: int = 0) -> dict:
    splits = jax.random.split(jax.random.key(seed), 5)
    return {
        "lagged": draw_lagged(jax.random.fold_in(splits[4], 71), 0),
        "weights": draw_weights(jax.random.fold_in(splits[4], 71), 0),
        "cell_index": draw_cell_index(jax.random.fold_in(splits[4], 71), 0),
        "fraction": jnp.clip(0.05 + 0.9 * jax.random.uniform(splits[3], (NCOL,), jnp.float32) ** block_scale(splits[3], (NCOL,), ((0, 32),), -0.2, 0.2), 0.05, 0.95),
    }


def reference(lagged, weights, cell_index, fraction):
    band_block = jnp.arange(NCOL, dtype=jnp.int32) // COLS
    left_point = ((band_block * GS + cell_index.astype(jnp.int32) - 1) % GC).astype(jnp.int32)
    right_point = ((left_point + 1) % GC).astype(jnp.int32)
    left_weight = weights[left_point]
    right_weight = weights[right_point]
    portion = fraction[:, None, None]
    blended = ((1.0 - portion) * left_weight + portion * right_weight).astype(jnp.bfloat16)
    blended = lax.optimization_barrier(blended)
    blended_wide_state = blended.astype(jnp.float32)

    def one_window(states):
        states_wide = states.astype(jnp.float32)
        center = jnp.mean(states_wide, axis=-1, keepdims=True)
        anomaly_spread = (states_wide - center).astype(jnp.bfloat16)
        anomaly_spread = lax.optimization_barrier(anomaly_spread)
        shifted_columns = jnp.einsum("pan,pnt->pat", anomaly_spread.astype(jnp.float32), blended_wide_state)
        return (center + shifted_columns).astype(jnp.bfloat16)

    return lax.map(one_window, lagged)
```

```python
import jax
import jax.numpy as jnp
from jax import lax
from jax.experimental import pallas as pl
from jax.experimental.pallas import tpu as pltpu
from jax.sharding import PartitionSpec as P

AXES = ("lag", "space")
BLOCK = 32


def send(block, step_x, step_z, step_space=0):
    lags, spaces = lax.axis_size("lag"), lax.axis_size("space")
    rows = lags // 2
    pairs = []
    for lag in range(lags):
        x, half = divmod(lag, 2)
        to = (x + step_x) % rows * 2 + (half + step_z) % 2
        shift = step_space[half] if step_space else 0
        pairs += [(lag * spaces + s, to * spaces + (s + shift) % spaces) for s in range(spaces)]
    return lax.ppermute(block, AXES, pairs)


def apply_kernel(me, cell, fraction, states_ref, *rest):
    parts, (left_ref, right_ref, out_ref, points) = rest[:8], rest[8:]
    size = parts[0].shape[0]
    step = pl.program_id(0)

    @pl.when(step == 0)
    def _():
        x, half = me[0] // 2, me[0] % 2
        for k, part in enumerate(parts):
            source = lax.rem(x + 4 - k % 4, 4) * 2 + lax.rem(half + k // 4, 2)
            points[pl.ds(1 + source * size, size)] = part[...]
        points[0] = left_ref[0]
        points[1 + 8 * size] = right_ref[0]

    def column(j, _):
        n = step * BLOCK + j
        c, f = cell[n], fraction[n]
        states = states_ref[j].astype(jnp.float32)
        center = jnp.mean(states, axis=-1, keepdims=True)
        spread = (states - center).astype(jnp.bfloat16)
        both = jnp.concatenate([points[c], points[c + 1]], axis=1)
        moved = jnp.dot(spread, both, preferred_element_type=jnp.float32)
        width = moved.shape[1] // 2
        out = center + (1.0 - f) * moved[:, :width] + f * moved[:, width:]
        out_ref[j] = out.astype(jnp.bfloat16)
        return 0

    lax.fori_loop(0, BLOCK, column, 0, unroll=True)


def shards(lagged, weights, cell_index, fraction):
    states = lagged[0]
    own = weights.astype(jnp.bfloat16)
    me = lax.axis_index("lag")
    x, half = me // 2, me % 2

    def along_x(block):
        return [block] + [send(block, k, 0) for k in (1, 2, 3)]

    across = send(own, 0, 1)
    same = along_x(own)
    other = along_x(across)
    held = jnp.where(half == 0, x, (x + 1) % 4)
    edges = [jnp.where(half == 0, p[:1], p[-1:]) for p in same]
    edge = jnp.where(held < 2, jnp.where(held == 0, edges[0], edges[1]), jnp.where(held == 2, edges[2], edges[3]))
    near = send(edge, 0, 0, (-1, 1))
    far = send(edge, 0, 1, (-1, 1))
    left = jnp.where(half == 0, far, near)
    right = jnp.where(half == 0, near, far)

    count, levels, members = states.shape
    block = pl.BlockSpec((BLOCK, levels, members), lambda i, *_: (i, 0, 0))
    whole = pl.BlockSpec(memory_space=pltpu.VMEM)
    points = 8 * own.shape[0] + 2
    smoothed = pl.pallas_call(
        apply_kernel,
        grid_spec=pltpu.PrefetchScalarGridSpec(
            num_scalar_prefetch=3,
            grid=(count // BLOCK,),
            in_specs=[block] + [whole] * 10,
            out_specs=block,
            scratch_shapes=[pltpu.VMEM((points, members, members), jnp.bfloat16)],
        ),
        out_shape=jax.ShapeDtypeStruct(states.shape, jnp.bfloat16),
        compiler_params=pltpu.CompilerParams(vmem_limit_bytes=24 << 20),
        cost_estimate=pl.CostEstimate(
            flops=4 * count * levels * members * members,
            bytes_accessed=4 * states.size,
            transcendentals=0,
        ),
    )(me.reshape(1), cell_index, fraction, states, *same, *other, left, right)
    return smoothed[None]


def solution(mesh):
    in_specs = (
        P("lag", "space", None, None),
        P(("space", "lag"), None, None),
        P("space"),
        P("space"),
    )
    out_specs = P("lag", "space", None, None)
    return jax.shard_map(shards, mesh=mesh, in_specs=in_specs, out_specs=out_specs, check_vma=False)
```
